32 devices in a mesh: dp: 8 (over z, y), tensor: 4 (over x, core).
Axes of the slice: x: 2, y: 2, z: 4, core: 2. Of those that a mesh axis runs over, the one named last changes fastest.
Arguments:
- tokens: bfloat16 [8, 256, 8192], P('dp', 'tensor'), may hold values from -6 to 6
- cotangent: bfloat16 [8, 256, 14336], P('dp', 'tensor'), may hold values from -6 to 6
- weights: bfloat16 [8, 112, 2, 2, 128, 128], P('dp', 'tensor'), may hold values from -6 to 6
- momentum: bfloat16 [8, 112, 2, 2, 128, 128], P('dp', 'tensor'), may hold values from -4 to 4
- pattern: int32 [112, 2], P('tensor'), may hold values from 0 to 63, all different within a row
- step: int32 [], replicated, may hold values from 0 to 4095
Outputs:
- hidden: bfloat16 [8, 256, 14336], P('dp', 'tensor')
- new_weights: bfloat16 [8, 112, 2, 2, 128, 128], P('dp', 'tensor')
- new_momentum: bfloat16 [8, 112, 2, 2, 128, 128], P('dp', 'tensor')
The draws below stay inside these ranges and needn't reach their ends.
Inputs may be any that keep to these rules, and one draw needn't show every extreme that they name: `pattern`: each row names 2 different input blocks; every input block is named by some row.
All inputs are finite; a program needn't handle non-finite values.
Results may differ from the reference program's by a relative error of at most 0.0058.
Values may be sent and summed in bfloat16 or wider, within the bound.
A program may use at most 128 MiB of HBM per device.

```python
from functools import partial
import jax
import jax.numpy as jnp
from jax import lax

D = 8192
FF = 14336
BLOCK = 128
KB = 2
TOKENS = 256
DB = 64
FFB = 112
N_DP = 8


def block_scale(stream_key, dims, split, low, high):
    def one(axis_at, parts):
        draws = jax.random.uniform(jax.random.fold_in(jax.random.fold_in(stream_key, 6), axis_at), (parts,), jnp.float32, low / len(split), high / len(split))
        return jnp.repeat(jnp.exp(draws), dims[axis_at] // parts).reshape((-1,) + (1,) * (len(dims) - axis_at - 1))

    loudness = one(*split[0])
    for cut in split[1:]:
        loudness = loudness * one(*cut)
    return loudness


def distinct(key, rows, number_of, top, lift):
    sequence = jax.random.permutation(jax.random.fold_in(key, 1), number_of)
    favour = sequence
    for power in range(3):
        favour = favour * favour // number_of
    favour = favour * lift // number_of
    chance = jax.random.randint(jax.random.fold_in(key, 2), (rows, number_of), 0, 4096) + favour
    sure = jax.random.permutation(jax.random.fold_in(key, 3), rows)[jnp.arange(number_of) % rows]
    chance = jnp.where(jnp.arange(rows)[:, None] == sure[None, :], 1 << 14, chance)
    score = chance * number_of + jnp.arange(number_of)
    return lax.top_k(score.astype(jnp.int32), top)[1].astype(jnp.int32)


def scatter_about(rng, extent, scale, limit, split=(), kind=jnp.bfloat16):
    drawn = jax.random.normal(rng, extent, jnp.float32) * scale
    if len(split) > 0:
        drawn = block_scale(rng, extent, split, -0.22, 0.18) * drawn
    return jnp.clip(drawn, min=-limit, max=limit).astype(kind)


def setup_inputs(seed: int = 0) -> dict:
    arg_keys = jax.random.split(jax.random.key(seed), 7)
    return {
        "tokens": scatter_about(arg_keys[0], (N_DP, TOKENS, D), 1.0, 6.0, ((0, 8), (1, 4))),
        "cotangent": scatter_about(arg_keys[1], (N_DP, TOKENS, FF), 1.0, 6.0, ((0, 8), (1, 4))),
        "weights": scatter_about(arg_keys[2], (N_DP, FFB, 2, KB, BLOCK, BLOCK), 1.0, 6.0, ((0, 8), (1, 4))),
        "momentum": scatter_about(arg_keys[3], (N_DP, FFB, 2, KB, BLOCK, BLOCK), 0.5, 4.0, ((0, 8), (1, 4))),
        "pattern": distinct(arg_keys[4], FFB, DB, KB, 0),
        "step": jax.random.randint(arg_keys[5], (), 0, 4096).astype(jnp.int32),
    }


def replica_step(pattern_flat, operands):
    tok_rows, cot_rows, packed, moment = operands
    scale = (KB * BLOCK) ** -0.5
    chosen = jnp.take(tok_rows.reshape(TOKENS, DB, BLOCK), pattern_flat, axis=1)
    chosen = chosen.reshape(TOKENS, FFB, KB, BLOCK).astype(jnp.float32)
    weights_f = packed.astype(jnp.float32)
    gate = jnp.einsum("rjkc,jkcf->rjf", chosen, weights_f[:, 0]) * scale
    up_val = jnp.einsum("rjkc,jkcf->rjf", chosen, weights_f[:, 1]) * scale
    sigma = jax.nn.sigmoid(gate)
    hidden = (gate * sigma * up_val).astype(jnp.bfloat16).reshape(TOKENS, FF)
    back = cot_rows.reshape(TOKENS, FFB, BLOCK).astype(jnp.float32)
    dgate = (back * up_val * sigma * (1.0 + gate * (1.0 - sigma))).astype(jnp.bfloat16)
    duptail = (back * gate * sigma).astype(jnp.bfloat16)
    grad_gate = jnp.einsum("rjkc,rjf->jkcf", chosen, dgate.astype(jnp.float32)) * scale
    grad_up = jnp.einsum("rjkc,rjf->jkcf", chosen, duptail.astype(jnp.float32)) * scale
    grad = jnp.stack([grad_gate, grad_up], axis=1)
    moved = (0.9 * moment.astype(jnp.float32) + grad).astype(jnp.bfloat16)
    stepped = (packed.astype(jnp.float32) - 0.1 * moved.astype(jnp.float32)).astype(jnp.bfloat16)
    return hidden, stepped, moved


def reference(tokens, cotangent, weights, momentum, pattern, step):
    pattern_flat = pattern.reshape(-1).astype(jnp.int32)
    hidden, stepped, moved = lax.map(partial(replica_step, pattern_flat), (tokens, cotangent, weights, momentum))
    levels = N_DP.bit_length() - 1
    distance = jnp.left_shift(jnp.int32(1), (step % levels).astype(jnp.int32))
    far_weights = jnp.roll(stepped, distance, axis=0)
    far_moment = jnp.roll(moved, distance, axis=0)
    new_weights = ((stepped.astype(jnp.float32) + far_weights.astype(jnp.float32)) * 0.5).astype(jnp.bfloat16)
    new_momentum = ((moved.astype(jnp.float32) + far_moment.astype(jnp.float32)) * 0.5).astype(jnp.bfloat16)
    return hidden, new_weights, new_momentum
```

```python
from functools import partial

import jax
import jax.numpy as jnp
from jax import lax
from jax.experimental import pallas as pl
from jax.experimental.pallas import tpu as pltpu
from jax.sharding import PartitionSpec as P

BLOCK = 128
KB = 2
SCALE = (KB * BLOCK) ** (-0.5)
MESH = pl.DeviceIdType.MESH


def stepped_of(packed, moved):
    return (packed.astype(jnp.float32) - 0.1 * moved.astype(jnp.float32)).astype(jnp.bfloat16)


def average(one, other):
    return ((one.astype(jnp.float32) + other.astype(jnp.float32)) * 0.5).astype(jnp.bfloat16)


def kernel(
    distance,
    replicas,
    groups,
    chunk,
    pat_ref,
    tok_ref,
    cot_ref,
    w_ref,
    m_ref,
    hid_out,
    nw_out,
    nm_out,
    tok_in,
    tok_mine,
    tok_all,
    cot_all,
    hid_all,
    w_own,
    m_own,
    w_far,
    m_far,
    in_sem,
    w_sem,
    m_send,
    m_recv,
    tok_send,
    tok_recv,
    cot_send,
    cot_recv,
    hid_send,
    hid_recv,
    out_sem,
):
    own_blocks = w_ref.shape[0]
    chunks = own_blocks // chunk
    rows = tok_ref.shape[0]
    input_blocks = tok_ref.shape[1] // BLOCK
    width = own_blocks * BLOCK
    seq = rows * groups
    here = lax.axis_index("tensor")
    replica = lax.axis_index("dp")
    ahead = {"dp": lax.rem(replica + distance, replicas)}
    behind = {"dp": lax.rem(replica + replicas - distance, replicas)}
    peers = [lax.rem(here + o, groups) for o in range(1, groups)]

    barrier = pltpu.get_barrier_semaphore()
    greeted = [{"tensor": q} for q in peers] + [ahead]
    if 2 * distance != replicas:
        greeted.append(behind)
    for device in greeted:
        pl.semaphore_signal(barrier, inc=1, device_id=device, device_id_type=MESH)

    def own_columns(q):
        return pl.ds(pl.multiple_of(q * width, BLOCK), width)

    loads = [
        pltpu.make_async_copy(tok_ref, tok_in, in_sem.at[0]),
        pltpu.make_async_copy(cot_ref.at[:, own_columns(here)], cot_all.at[here], in_sem.at[1]),
        pltpu.make_async_copy(w_ref, w_own, in_sem.at[2]),
        pltpu.make_async_copy(m_ref, m_own, in_sem.at[3]),
    ]
    for load in loads:
        load.start()
    pl.semaphore_wait(barrier, len(greeted))

    tok_copies = [
        pltpu.make_async_remote_copy(
            src_ref=tok_mine,
            dst_ref=tok_all.at[:, here],
            send_sem=tok_send.at[i],
            recv_sem=tok_recv.at[i],
            device_id={"tensor": q},
            device_id_type=MESH,
        )
        for i, q in enumerate(peers)
    ]
    cot_copies = [
        pltpu.make_async_remote_copy(
            src_ref=cot_ref.at[:, own_columns(q)],
            dst_ref=cot_all.at[here],
            send_sem=cot_send.at[i],
            recv_sem=cot_recv.at[i],
            device_id={"tensor": q},
            device_id_type=MESH,
        )
        for i, q in enumerate(peers)
    ]
    w_copy = pltpu.make_async_remote_copy(
        src_ref=w_ref,
        dst_ref=w_far,
        send_sem=w_sem.at[0],
        recv_sem=w_sem.at[1],
        device_id=ahead,
        device_id_type=MESH,
    )
    w_copy.start()
    loads[0].wait()
    for b in range(input_blocks):
        tok_mine[b] = tok_in[:, b * BLOCK : (b + 1) * BLOCK]
    for copy in tok_copies:
        copy.start()
    for copy in cot_copies:
        copy.start()
    tok_own = pltpu.make_async_copy(tok_mine, tok_all.at[:, here], in_sem.at[0])
    tok_own.start()
    for load in loads[1:] + [tok_own]:
        load.wait()
    for copy in tok_copies + cot_copies:
        copy.wait()

    def moved_copy(c):
        part = pl.ds(c * chunk, chunk)
        return pltpu.make_async_remote_copy(
            src_ref=m_own.at[part],
            dst_ref=m_far.at[part],
            send_sem=m_send.at[c],
            recv_sem=m_recv.at[c],
            device_id=ahead,
            device_id_type=MESH,
        )

    def make_block(j):
        cols = pl.ds(pl.multiple_of(j * BLOCK, BLOCK), BLOCK)
        chosen = jnp.concatenate(
            [tok_all[pat_ref[j, k]].reshape(seq, BLOCK) for k in range(KB)], axis=1
        )
        packed = jnp.concatenate(
            [w_own[j, u].reshape(KB * BLOCK, BLOCK) for u in range(2)], axis=1
        )
        both = jnp.dot(chosen, packed, preferred_element_type=jnp.float32) * SCALE
        gate, up = both[:, :BLOCK], both[:, BLOCK:]
        sigma = jax.nn.sigmoid(gate)
        gated = gate * sigma
        hid_all[:, :, cols] = (gated * up).astype(jnp.bfloat16).reshape(groups, rows, BLOCK)
        back = cot_all[:, :, cols].reshape(seq, BLOCK).astype(jnp.float32)
        dgate = (back * up * sigma * (1.0 + gate * (1.0 - sigma))).astype(jnp.bfloat16)
        duptail = (back * gated).astype(jnp.bfloat16)
        tails = jnp.concatenate([dgate, duptail], axis=1)
        grad = (
            lax.dot_general(
                chosen, tails, (((0,), (0,)), ((), ())), preferred_element_type=jnp.float32
            )
            * SCALE
        )
        for u in range(2):
            old = m_own[j, u].reshape(KB * BLOCK, BLOCK).astype(jnp.float32)
            new = (0.9 * old + grad[:, u * BLOCK : (u + 1) * BLOCK]).astype(jnp.bfloat16)
            m_own[j, u] = new.reshape(KB, BLOCK, BLOCK)

    def make_chunk(c, carry):
        for i in range(chunk):
            make_block(c * chunk + i)
        moved_copy(c).start()
        return carry

    lax.fori_loop(0, chunks, make_chunk, 0)

    hid_copies = [
        pltpu.make_async_remote_copy(
            src_ref=hid_all.at[q],
            dst_ref=hid_out.at[:, own_columns(here)],
            send_sem=hid_send.at[i],
            recv_sem=hid_recv.at[i],
            device_id={"tensor": q},
            device_id_type=MESH,
        )
        for i, q in enumerate(peers)
    ]
    for copy in hid_copies:
        copy.start()
    hid_own = pltpu.make_async_copy(
        hid_all.at[here], hid_out.at[:, own_columns(here)], in_sem.at[0]
    )
    hid_own.start()

    def out_copies(c):
        part = pl.ds(c * chunk, chunk)
        return (
            pltpu.make_async_copy(w_far.at[part], nw_out.at[part], out_sem.at[0, c]),
            pltpu.make_async_copy(m_far.at[part], nm_out.at[part], out_sem.at[1, c]),
        )

    w_copy.wait()

    def mix_chunk(c, carry):
        moved_copy(c).wait_recv()
        for i in range(chunk):
            j = c * chunk + i
            moved, far_moved = m_own[j], m_far[j]
            w_far[j] = average(stepped_of(w_own[j], moved), stepped_of(w_far[j], far_moved))
            m_far[j] = average(moved, far_moved)
        for copy in out_copies(c):
            copy.start()
        return carry

    lax.fori_loop(0, chunks, mix_chunk, 0)

    def finish_chunk(c, carry):
        moved_copy(c).wait_send()
        for copy in out_copies(c):
            copy.wait()
        return carry

    lax.fori_loop(0, chunks, finish_chunk, 0)
    for copy in hid_copies:
        copy.wait()
    hid_own.wait()


def run(distance, replicas, groups, number, pattern, tokens, cotangent, weights, momentum):
    rows, model = tokens.shape
    own_blocks = weights.shape[0]
    width = own_blocks * BLOCK
    chunk = 2 if own_blocks % 2 == 0 else 1
    chunks = own_blocks // chunk
    bf16 = jnp.bfloat16
    anywhere = pl.BlockSpec(memory_space=pl.ANY)
    others = groups - 1
    dma = pltpu.SemaphoreType.DMA
    return pl.pallas_call(
        partial(kernel, distance, replicas, groups, chunk),
        out_shape=(
            jax.ShapeDtypeStruct(cotangent.shape, bf16),
            jax.ShapeDtypeStruct(weights.shape, bf16),
            jax.ShapeDtypeStruct(weights.shape, bf16),
        ),
        in_specs=[pl.BlockSpec(memory_space=pltpu.SMEM)] + [anywhere] * 4,
        out_specs=(anywhere,) * 3,
        scratch_shapes=[
            pltpu.VMEM((rows, model), bf16),
            pltpu.VMEM((model // BLOCK, rows, BLOCK), bf16),
            pltpu.VMEM((model // BLOCK, groups, rows, BLOCK), bf16),
            pltpu.VMEM((groups, rows, width), bf16),
            pltpu.VMEM((groups, rows, width), bf16),
            pltpu.VMEM(weights.shape, bf16),
            pltpu.VMEM(weights.shape, bf16),
            pltpu.VMEM(weights.shape, bf16),
            pltpu.VMEM(weights.shape, bf16),
            dma((4,)),
            dma((2,)),
            dma((chunks,)),
            dma((chunks,)),
            dma((others,)),
            dma((others,)),
            dma((others,)),
            dma((others,)),
            dma((others,)),
            dma((others,)),
            dma((2, chunks)),
        ],
        compiler_params=pltpu.CompilerParams(
            collective_id=number, has_side_effects=True, vmem_limit_bytes=52 * 1024 * 1024
        ),
        cost_estimate=pl.CostEstimate(
            flops=8 * groups * rows * KB * BLOCK * width,
            bytes_accessed=2 * (groups * rows * model + 6 * weights.size),
            transcendentals=groups * rows * width,
        ),
    )(pattern, tokens, cotangent, weights, momentum)


def per_device(tokens, cotangent, weights, momentum, pattern, step):
    replicas = lax.axis_size("dp")
    groups = lax.axis_size("tensor")
    levels = replicas.bit_length() - 1
    branches = [partial(run, 2**level, replicas, groups, level) for level in range(levels)]
    hidden, new_weights, new_momentum = lax.switch(
        step % levels, branches, pattern, tokens[0], cotangent[0], weights[0], momentum[0]
    )
    return (hidden[None], new_weights[None], new_momentum[None])


def solution(mesh):
    in_specs = (
        P("dp", "tensor", None),
        P("dp", "tensor", None),
        P("dp", "tensor", None, None, None, None),
        P("dp", "tensor", None, None, None, None),
        P("tensor", None),
        P(),
    )
    out_specs = (
        P("dp", "tensor", None),
        P("dp", "tensor", None, None, None, None),
        P("dp", "tensor", None, None, None, None),
    )
    return jax.shard_map(
        per_device, mesh=mesh, in_specs=in_specs, out_specs=out_specs, check_vma=False
    )
```

```python
from functools import partial

import jax
import jax.numpy as jnp
from jax import lax
from jax.experimental import pallas as pl
from jax.experimental.pallas import tpu as pltpu
from jax.sharding import PartitionSpec as P

BLOCK = 128
KB = 2
SCALE = (KB * BLOCK) ** (-0.5)
MESH = pl.DeviceIdType.MESH


def stepped_of(packed, moved):
    return (packed.astype(jnp.float32) - 0.1 * moved.astype(jnp.float32)).astype(jnp.bfloat16)


def average(one, other):
    return ((one.astype(jnp.float32) + other.astype(jnp.float32)) * 0.5).astype(jnp.bfloat16)


def kernel(
    distance,
    replicas,
    groups,
    chunk,
    pat_hbm,
    tok_ref,
    cot_ref,
    w_ref,
    m_ref,
    hid_out,
    nw_out,
    nm_out,
    tok_in,
    tok_mine,
    tok_all,
    cot_all,
    hid_all,
    w_own,
    m_own,
    w_far,
    m_far,
    pat_ref,
    in_sem,
    w_sem,
    m_send,
    m_recv,
    tok_send,
    tok_recv,
    cot_send,
    cot_recv,
    hid_send,
    hid_recv,
    out_sem,
):
    own_blocks = w_ref.shape[0]
    chunks = own_blocks // chunk
    rows = tok_ref.shape[0]
    input_blocks = tok_ref.shape[1] // BLOCK
    width = own_blocks * BLOCK
    seq = rows * groups
    here = lax.axis_index("tensor")
    replica = lax.axis_index("dp")
    ahead = {"dp": lax.rem(replica + distance, replicas)}
    behind = {"dp": lax.rem(replica + replicas - distance, replicas)}
    peers = [lax.rem(here + o, groups) for o in range(1, groups)]

    barrier = pltpu.get_barrier_semaphore()
    greeted = [{"tensor": q} for q in peers] + [ahead]
    if 2 * distance != replicas:
        greeted.append(behind)
    for device in greeted:
        pl.semaphore_signal(barrier, inc=1, device_id=device, device_id_type=MESH)

    def own_columns(q):
        return pl.ds(pl.multiple_of(q * width, BLOCK), width)

    loads = [
        pltpu.make_async_copy(tok_ref, tok_in, in_sem.at[0]),
        pltpu.make_async_copy(cot_ref.at[:, own_columns(here)], cot_all.at[here], in_sem.at[1]),
        pltpu.make_async_copy(w_ref, w_own, in_sem.at[2]),
        pltpu.make_async_copy(m_ref, m_own, in_sem.at[3]),
        pltpu.make_async_copy(pat_hbm, pat_ref, in_sem.at[4]),
    ]
    for load in loads:
        load.start()
    pl.semaphore_wait(barrier, len(greeted))

    tok_copies = [
        pltpu.make_async_remote_copy(
            src_ref=tok_mine,
            dst_ref=tok_all.at[:, here],
            send_sem=tok_send.at[i],
            recv_sem=tok_recv.at[i],
            device_id={"tensor": q},
            device_id_type=MESH,
        )
        for i, q in enumerate(peers)
    ]
    cot_copies = [
        pltpu.make_async_remote_copy(
            src_ref=cot_ref.at[:, own_columns(q)],
            dst_ref=cot_all.at[here],
            send_sem=cot_send.at[i],
            recv_sem=cot_recv.at[i],
            device_id={"tensor": q},
            device_id_type=MESH,
        )
        for i, q in enumerate(peers)
    ]
    w_copy = pltpu.make_async_remote_copy(
        src_ref=w_ref,
        dst_ref=w_far,
        send_sem=w_sem.at[0],
        recv_sem=w_sem.at[1],
        device_id=ahead,
        device_id_type=MESH,
    )
    w_copy.start()
    loads[0].wait()
    for b in range(input_blocks):
        tok_mine[b] = tok_in[:, b * BLOCK : (b + 1) * BLOCK]
    for copy in tok_copies:
        copy.start()
    for copy in cot_copies:
        copy.start()
    tok_own = pltpu.make_async_copy(tok_mine, tok_all.at[:, here], in_sem.at[0])
    tok_own.start()
    for load in loads[1:] + [tok_own]:
        load.wait()
    for copy in tok_copies + cot_copies:
        copy.wait()

    def moved_copy(c):
        part = pl.ds(c * chunk, chunk)
        return pltpu.make_async_remote_copy(
            src_ref=m_own.at[part],
            dst_ref=m_far.at[part],
            send_sem=m_send.at[c],
            recv_sem=m_recv.at[c],
            device_id=ahead,
            device_id_type=MESH,
        )

    def make_block(j):
        cols = pl.ds(pl.multiple_of(j * BLOCK, BLOCK), BLOCK)
        chosen = jnp.concatenate(
            [tok_all[pat_ref[k, j]].reshape(seq, BLOCK) for k in range(KB)], axis=1
        )
        packed = jnp.concatenate(
            [w_own[j, u].reshape(KB * BLOCK, BLOCK) for u in range(2)], axis=1
        )
        both = jnp.dot(chosen, packed, preferred_element_type=jnp.float32) * SCALE
        gate, up = both[:, :BLOCK], both[:, BLOCK:]
        sigma = jax.nn.sigmoid(gate)
        gated = gate * sigma
        hid_all[:, :, cols] = (gated * up).astype(jnp.bfloat16).reshape(groups, rows, BLOCK)
        back = cot_all[:, :, cols].reshape(seq, BLOCK).astype(jnp.float32)
        dgate = (back * up * sigma * (1.0 + gate * (1.0 - sigma))).astype(jnp.bfloat16)
        duptail = (back * gated).astype(jnp.bfloat16)
        tails = jnp.concatenate([dgate, duptail], axis=1)
        grad = (
            lax.dot_general(
                chosen, tails, (((0,), (0,)), ((), ())), preferred_element_type=jnp.float32
            )
            * SCALE
        )
        for u in range(2):
            old = m_own[j, u].reshape(KB * BLOCK, BLOCK).astype(jnp.float32)
            new = (0.9 * old + grad[:, u * BLOCK : (u + 1) * BLOCK]).astype(jnp.bfloat16)
            m_own[j, u] = new.reshape(KB, BLOCK, BLOCK)

    def make_chunk(c, carry):
        for i in range(chunk):
            make_block(c * chunk + i)
        moved_copy(c).start()
        return carry

    lax.fori_loop(0, chunks, make_chunk, 0)

    hid_copies = [
        pltpu.make_async_remote_copy(
            src_ref=hid_all.at[q],
            dst_ref=hid_out.at[:, own_columns(here)],
            send_sem=hid_send.at[i],
            recv_sem=hid_recv.at[i],
            device_id={"tensor": q},
            device_id_type=MESH,
        )
        for i, q in enumerate(peers)
    ]
    for copy in hid_copies:
        copy.start()
    hid_own = pltpu.make_async_copy(
        hid_all.at[here], hid_out.at[:, own_columns(here)], in_sem.at[0]
    )
    hid_own.start()

    def out_copies(c):
        part = pl.ds(c * chunk, chunk)
        return (
            pltpu.make_async_copy(w_far.at[part], nw_out.at[part], out_sem.at[0, c]),
            pltpu.make_async_copy(m_far.at[part], nm_out.at[part], out_sem.at[1, c]),
        )

    w_copy.wait()

    def mix_chunk(c, carry):
        moved_copy(c).wait_recv()
        for i in range(chunk):
            j = c * chunk + i
            moved, far_moved = m_own[j], m_far[j]
            w_far[j] = average(stepped_of(w_own[j], moved), stepped_of(w_far[j], far_moved))
            m_far[j] = average(moved, far_moved)
        for copy in out_copies(c):
            copy.start()
        return carry

    lax.fori_loop(0, chunks, mix_chunk, 0)

    def finish_chunk(c, carry):
        moved_copy(c).wait_send()
        for copy in out_copies(c):
            copy.wait()
        return carry

    lax.fori_loop(0, chunks, finish_chunk, 0)
    for copy in hid_copies:
        copy.wait()
    hid_own.wait()


def run(distance, replicas, groups, number, pattern, tokens, cotangent, weights, momentum):
    rows, model = tokens.shape
    own_blocks = weights.shape[0]
    width = own_blocks * BLOCK
    chunk = 2 if own_blocks % 2 == 0 else 1
    chunks = own_blocks // chunk
    bf16 = jnp.bfloat16
    anywhere = pl.BlockSpec(memory_space=pl.ANY)
    others = groups - 1
    dma = pltpu.SemaphoreType.DMA
    return pl.pallas_call(
        partial(kernel, distance, replicas, groups, chunk),
        out_shape=(
            jax.ShapeDtypeStruct(cotangent.shape, bf16),
            jax.ShapeDtypeStruct(weights.shape, bf16),
            jax.ShapeDtypeStruct(weights.shape, bf16),
        ),
        in_specs=[anywhere] * 5,
        out_specs=(anywhere,) * 3,
        scratch_shapes=[
            pltpu.VMEM((rows, model), bf16),
            pltpu.VMEM((model // BLOCK, rows, BLOCK), bf16),
            pltpu.VMEM((model // BLOCK, groups, rows, BLOCK), bf16),
            pltpu.VMEM((groups, rows, width), bf16),
            pltpu.VMEM((groups, rows, width), bf16),
            pltpu.VMEM(weights.shape, bf16),
            pltpu.VMEM(weights.shape, bf16),
            pltpu.VMEM(weights.shape, bf16),
            pltpu.VMEM(weights.shape, bf16),
            pltpu.SMEM(pattern.shape, jnp.int32),
            dma((5,)),
            dma((2,)),
            dma((chunks,)),
            dma((chunks,)),
            dma((others,)),
            dma((others,)),
            dma((others,)),
            dma((others,)),
            dma((others,)),
            dma((others,)),
            dma((2, chunks)),
        ],
        compiler_params=pltpu.CompilerParams(
            collective_id=number, has_side_effects=True, vmem_limit_bytes=52 * 1024 * 1024
        ),
        cost_estimate=pl.CostEstimate(
            flops=8 * groups * rows * KB * BLOCK * width,
            bytes_accessed=2 * (groups * rows * model + 6 * weights.size),
            transcendentals=groups * rows * width,
        ),
    )(pattern, tokens, cotangent, weights, momentum)


def write_kernel(hid_ref, nw_ref, nm_ref, hid_out, nw_out, nm_out, sems):
    pairs = ((hid_ref, hid_out), (nw_ref, nw_out), (nm_ref, nm_out))
    copies = []
    for i, (src, dst) in enumerate(pairs):
        half = src.shape[0] // 2
        for k in range(2):
            part = pl.ds(k * half, half)
            copies.append(pltpu.make_async_copy(src.at[part], dst.at[part], sems.at[i, k]))
    for copy in copies:
        copy.start()
    for copy in copies:
        copy.wait()


def written(*results):
    return pl.pallas_call(
        write_kernel,
        out_shape=tuple(jax.ShapeDtypeStruct(r.shape, r.dtype) for r in results),
        in_specs=[pl.BlockSpec(memory_space=pl.ANY)] * len(results),
        out_specs=(pl.BlockSpec(memory_space=pltpu.HBM),) * len(results),
        scratch_shapes=[pltpu.SemaphoreType.DMA((len(results), 2))],
        compiler_params=pltpu.CompilerParams(vmem_limit_bytes=1024 * 1024),
    )(*results)


def per_device(tokens, cotangent, weights, momentum, pattern, step):
    replicas = lax.axis_size("dp")
    groups = lax.axis_size("tensor")
    levels = replicas.bit_length() - 1
    branches = [partial(run, 2**level, replicas, groups, level) for level in range(levels)]
    hidden, new_weights, new_momentum = lax.switch(
        step % levels, branches, pattern.T, tokens[0], cotangent[0], weights[0], momentum[0]
    )
    hidden, new_weights, new_momentum = written(hidden, new_weights, new_momentum)
    return (hidden[None], new_weights[None], new_momentum[None])


def solution(mesh):
    in_specs = (
        P("dp", "tensor", None),
        P("dp", "tensor", None),
        P("dp", "tensor", None, None, None, None),
        P("dp", "tensor", None, None, None, None),
        P("tensor", None),
        P(),
    )
    out_specs = (
        P("dp", "tensor", None),
        P("dp", "tensor", None, None, None, None),
        P("dp", "tensor", None, None, None, None),
    )
    return jax.shard_map(
        per_device, mesh=mesh, in_specs=in_specs, out_specs=out_specs, check_vma=False
    )
```

```python
from functools import partial

import jax
import jax.numpy as jnp
from jax import lax
from jax.experimental import pallas as pl
from jax.experimental.pallas import tpu as pltpu
from jax.sharding import PartitionSpec as P

BLOCK = 128
KB = 2
SCALE = (KB * BLOCK) ** (-0.5)
MESH = pl.DeviceIdType.MESH
FIRST = 10
AHEAD = 4


def stepped_of(packed, moved):
    return (packed.astype(jnp.float32) - 0.1 * moved.astype(jnp.float32)).astype(jnp.bfloat16)


def average(one, other):
    return ((one.astype(jnp.float32) + other.astype(jnp.float32)) * 0.5).astype(jnp.bfloat16)


def kernel(
    distance,
    replicas,
    groups,
    pat_hbm,
    tok_ref,
    cot_ref,
    w_ref,
    m_ref,
    hid_out,
    nw_out,
    nm_out,
    tok_in,
    tok_mine,
    tok_all,
    cot_all,
    hid_all,
    w_own,
    m_own,
    w_far,
    m_far,
    pat_ref,
    in_sem,
    w_sem,
    m_send,
    m_recv,
    tok_send,
    tok_recv,
    cot_send,
    cot_recv,
    hid_send,
    hid_recv,
    out_sem,
):
    own_blocks = w_ref.shape[0]
    rows = tok_ref.shape[0]
    input_blocks = tok_ref.shape[1] // BLOCK
    width = own_blocks * BLOCK
    seq = rows * groups
    here = lax.axis_index("tensor")
    replica = lax.axis_index("dp")
    ahead = {"dp": lax.rem(replica + distance, replicas)}
    behind = {"dp": lax.rem(replica + replicas - distance, replicas)}
    peers = [lax.rem(here + o, groups) for o in range(1, groups)]

    barrier = pltpu.get_barrier_semaphore()
    greeted = [{"tensor": q} for q in peers] + [ahead]
    if 2 * distance != replicas:
        greeted.append(behind)
    for device in greeted:
        pl.semaphore_signal(barrier, inc=1, device_id=device, device_id_type=MESH)

    def own_columns(q):
        return pl.ds(pl.multiple_of(q * width, BLOCK), width)

    loads = [
        pltpu.make_async_copy(tok_ref, tok_in, in_sem.at[0]),
        pltpu.make_async_copy(cot_ref.at[:, own_columns(here)], cot_all.at[here], in_sem.at[1]),
        pltpu.make_async_copy(w_ref, w_own, in_sem.at[2]),
        pltpu.make_async_copy(m_ref, m_own, in_sem.at[3]),
        pltpu.make_async_copy(pat_hbm, pat_ref, in_sem.at[4]),
    ]
    for load in loads:
        load.start()
    pl.semaphore_wait(barrier, len(greeted))

    tok_copies = [
        pltpu.make_async_remote_copy(
            src_ref=tok_mine,
            dst_ref=tok_all.at[:, here],
            send_sem=tok_send.at[i],
            recv_sem=tok_recv.at[i],
            device_id={"tensor": q},
            device_id_type=MESH,
        )
        for i, q in enumerate(peers)
    ]
    cot_copies = [
        pltpu.make_async_remote_copy(
            src_ref=cot_ref.at[:, own_columns(q)],
            dst_ref=cot_all.at[here],
            send_sem=cot_send.at[i],
            recv_sem=cot_recv.at[i],
            device_id={"tensor": q},
            device_id_type=MESH,
        )
        for i, q in enumerate(peers)
    ]
    w_copy = pltpu.make_async_remote_copy(
        src_ref=w_ref,
        dst_ref=w_far,
        send_sem=w_sem.at[0],
        recv_sem=w_sem.at[1],
        device_id=ahead,
        device_id_type=MESH,
    )
    w_copy.start()
    loads[0].wait()
    for b in range(input_blocks):
        tok_mine[b] = tok_in[:, b * BLOCK : (b + 1) * BLOCK]
    for copy in tok_copies:
        copy.start()
    for copy in cot_copies:
        copy.start()
    tok_own = pltpu.make_async_copy(tok_mine, tok_all.at[:, here], in_sem.at[0])
    tok_own.start()
    for load in loads[1:] + [tok_own]:
        load.wait()
    for copy in tok_copies + cot_copies:
        copy.wait()

    def moved_copy(j):
        return pltpu.make_async_remote_copy(
            src_ref=m_own.at[j],
            dst_ref=m_far.at[j],
            send_sem=m_send.at[j],
            recv_sem=m_recv.at[j],
            device_id=ahead,
            device_id_type=MESH,
        )

    def make_block(j):
        cols = pl.ds(pl.multiple_of(j * BLOCK, BLOCK), BLOCK)
        chosen = jnp.concatenate(
            [tok_all[pat_ref[k, j]].reshape(seq, BLOCK) for k in range(KB)], axis=1
        )
        packed = jnp.concatenate(
            [w_own[j, u].reshape(KB * BLOCK, BLOCK) for u in range(2)], axis=1
        )
        both = jnp.dot(chosen, packed, preferred_element_type=jnp.float32) * SCALE
        gate, up = both[:, :BLOCK], both[:, BLOCK:]
        sigma = jax.nn.sigmoid(gate)
        gated = gate * sigma
        hid_all[:, :, cols] = (gated * up).astype(jnp.bfloat16).reshape(groups, rows, BLOCK)
        back = cot_all[:, :, cols].reshape(seq, BLOCK).astype(jnp.float32)
        dgate = (back * up * sigma * (1.0 + gate * (1.0 - sigma))).astype(jnp.bfloat16)
        duptail = (back * gated).astype(jnp.bfloat16)
        tails = jnp.concatenate([dgate, duptail], axis=1)
        grad = (
            lax.dot_general(
                chosen, tails, (((0,), (0,)), ((), ())), preferred_element_type=jnp.float32
            )
            * SCALE
        )
        for u in range(2):
            old = m_own[j, u].reshape(KB * BLOCK, BLOCK).astype(jnp.float32)
            new = (0.9 * old + grad[:, u * BLOCK : (u + 1) * BLOCK]).astype(jnp.bfloat16)
            m_own[j, u] = new.reshape(KB, BLOCK, BLOCK)

    burst = min(FIRST, own_blocks)

    def make_and_send(j, carry):
        make_block(j)
        moved_copy(j).start()
        return carry

    def make_only(j, carry):
        make_block(j)
        return carry

    lax.fori_loop(0, burst, make_and_send, 0)
    lax.fori_loop(burst, own_blocks, make_only, 0)

    hid_copies = [
        pltpu.make_async_remote_copy(
            src_ref=hid_all.at[q],
            dst_ref=hid_out.at[:, own_columns(here)],
            send_sem=hid_send.at[i],
            recv_sem=hid_recv.at[i],
            device_id={"tensor": q},
            device_id_type=MESH,
        )
        for i, q in enumerate(peers)
    ]
    for copy in hid_copies:
        copy.start()
    hid_own = pltpu.make_async_copy(
        hid_all.at[here], hid_out.at[:, own_columns(here)], in_sem.at[0]
    )
    hid_own.start()

    def out_copies(j):
        return (
            pltpu.make_async_copy(w_far.at[j], nw_out.at[j], out_sem.at[0, j]),
            pltpu.make_async_copy(m_far.at[j], nm_out.at[j], out_sem.at[1, j]),
        )

    w_copy.wait()

    def mix_block(j, carry):
        moved_copy(j).wait_send()
        later = j + AHEAD

        @pl.when(jnp.logical_and(later >= burst, later < own_blocks))
        def _():
            moved_copy(later).start()

        moved_copy(j).wait_recv()
        moved, far_moved = m_own[j], m_far[j]
        w_far[j] = average(stepped_of(w_own[j], moved), stepped_of(w_far[j], far_moved))
        m_far[j] = average(moved, far_moved)
        for copy in out_copies(j):
            copy.start()
        return carry

    lax.fori_loop(0, own_blocks, mix_block, 0)

    def finish_block(j, carry):
        for copy in out_copies(j):
            copy.wait()
        return carry

    lax.fori_loop(0, own_blocks, finish_block, 0)
    for copy in hid_copies:
        copy.wait()
    hid_own.wait()


def run(distance, replicas, groups, number, pattern, tokens, cotangent, weights, momentum):
    rows, model = tokens.shape
    own_blocks = weights.shape[0]
    width = own_blocks * BLOCK
    bf16 = jnp.bfloat16
    anywhere = pl.BlockSpec(memory_space=pl.ANY)
    others = groups - 1
    dma = pltpu.SemaphoreType.DMA
    return pl.pallas_call(
        partial(kernel, distance, replicas, groups),
        out_shape=(
            jax.ShapeDtypeStruct(cotangent.shape, bf16),
            jax.ShapeDtypeStruct(weights.shape, bf16),
            jax.ShapeDtypeStruct(weights.shape, bf16),
        ),
        in_specs=[anywhere] * 5,
        out_specs=(anywhere,) * 3,
        scratch_shapes=[
            pltpu.VMEM((rows, model), bf16),
            pltpu.VMEM((model // BLOCK, rows, BLOCK), bf16),
            pltpu.VMEM((model // BLOCK, groups, rows, BLOCK), bf16),
            pltpu.VMEM((groups, rows, width), bf16),
            pltpu.VMEM((groups, rows, width), bf16),
            pltpu.VMEM(weights.shape, bf16),
            pltpu.VMEM(weights.shape, bf16),
            pltpu.VMEM(weights.shape, bf16),
            pltpu.VMEM(weights.shape, bf16),
            pltpu.SMEM(pattern.shape, jnp.int32),
            dma((5,)),
            dma((2,)),
            dma((own_blocks,)),
            dma((own_blocks,)),
            dma((others,)),
            dma((others,)),
            dma((others,)),
            dma((others,)),
            dma((others,)),
            dma((others,)),
            dma((2, own_blocks)),
        ],
        compiler_params=pltpu.CompilerParams(
            collective_id=number, has_side_effects=True, vmem_limit_bytes=52 * 1024 * 1024
        ),
        cost_estimate=pl.CostEstimate(
            flops=8 * groups * rows * KB * BLOCK * width,
            bytes_accessed=2 * (groups * rows * model + 6 * weights.size),
            transcendentals=groups * rows * width,
        ),
    )(pattern, tokens, cotangent, weights, momentum)


def per_device(tokens, cotangent, weights, momentum, pattern, step):
    replicas = lax.axis_size("dp")
    groups = lax.axis_size("tensor")
    levels = replicas.bit_length() - 1
    branches = [partial(run, 2**level, replicas, groups, level) for level in range(levels)]
    hidden, new_weights, new_momentum = lax.switch(
        step % levels, branches, pattern.T, tokens[0], cotangent[0], weights[0], momentum[0]
    )
    return (hidden[None], new_weights[None], new_momentum[None])


def solution(mesh):
    in_specs = (
        P("dp", "tensor", None),
        P("dp", "tensor", None),
        P("dp", "tensor", None, None, None, None),
        P("dp", "tensor", None, None, None, None),
        P("tensor", None),
        P(),
    )
    out_specs = (
        P("dp", "tensor", None),
        P("dp", "tensor", None, None, None, None),
        P("dp", "tensor", None, None, None, None),
    )
    return jax.shard_map(
        per_device, mesh=mesh, in_specs=in_specs, out_specs=out_specs, check_vma=False
    )
```

```python
from functools import partial

import jax
import jax.numpy as jnp
from jax import lax
from jax.experimental import pallas as pl
from jax.experimental.pallas import tpu as pltpu
from jax.sharding import PartitionSpec as P

BLOCK = 128
KB = 2
SCALE = (KB * BLOCK) ** (-0.5)
MESH = pl.DeviceIdType.MESH
FIRST = 10
AHEAD = 4


def stepped_of(packed, moved):
    return (packed.astype(jnp.float32) - 0.1 * moved.astype(jnp.float32)).astype(jnp.bfloat16)


def average(one, other):
    return ((one.astype(jnp.float32) + other.astype(jnp.float32)) * 0.5).astype(jnp.bfloat16)


def kernel(
    distance,
    replicas,
    groups,
    pat_hbm,
    tok_ref,
    cot_ref,
    w_ref,
    m_ref,
    hid_out,
    nw_out,
    nm_out,
    tok_in,
    tok_mine,
    tok_all,
    cot_all,
    hid_all,
    w_own,
    m_own,
    w_far,
    m_far,
    pat_ref,
    in_sem,
    w_sem,
    m_send,
    m_recv,
    tok_send,
    tok_recv,
    cot_send,
    cot_recv,
    hid_send,
    hid_recv,
):
    own_blocks = w_ref.shape[0]
    rows = tok_ref.shape[0]
    input_blocks = tok_ref.shape[1] // BLOCK
    width = own_blocks * BLOCK
    seq = rows * groups
    here = lax.axis_index("tensor")
    replica = lax.axis_index("dp")
    ahead = {"dp": lax.rem(replica + distance, replicas)}
    behind = {"dp": lax.rem(replica + replicas - distance, replicas)}
    peers = [lax.rem(here + o, groups) for o in range(1, groups)]

    barrier = pltpu.get_barrier_semaphore()
    greeted = [{"tensor": q} for q in peers] + [ahead]
    if 2 * distance != replicas:
        greeted.append(behind)
    for device in greeted:
        pl.semaphore_signal(barrier, inc=1, device_id=device, device_id_type=MESH)

    def own_columns(q):
        return pl.ds(pl.multiple_of(q * width, BLOCK), width)

    loads = [
        pltpu.make_async_copy(tok_ref, tok_in, in_sem.at[0]),
        pltpu.make_async_copy(cot_ref.at[:, own_columns(here)], cot_all.at[here], in_sem.at[1]),
        pltpu.make_async_copy(w_ref, w_own, in_sem.at[2]),
        pltpu.make_async_copy(m_ref, m_own, in_sem.at[3]),
        pltpu.make_async_copy(pat_hbm, pat_ref, in_sem.at[4]),
    ]
    for load in loads:
        load.start()
    pl.semaphore_wait(barrier, len(greeted))

    tok_copies = [
        pltpu.make_async_remote_copy(
            src_ref=tok_mine,
            dst_ref=tok_all.at[:, here],
            send_sem=tok_send.at[i],
            recv_sem=tok_recv.at[i],
            device_id={"tensor": q},
            device_id_type=MESH,
        )
        for i, q in enumerate(peers)
    ]
    cot_copies = [
        pltpu.make_async_remote_copy(
            src_ref=cot_ref.at[:, own_columns(q)],
            dst_ref=cot_all.at[here],
            send_sem=cot_send.at[i],
            recv_sem=cot_recv.at[i],
            device_id={"tensor": q},
            device_id_type=MESH,
        )
        for i, q in enumerate(peers)
    ]
    w_copy = pltpu.make_async_remote_copy(
        src_ref=w_ref,
        dst_ref=w_far,
        send_sem=w_sem.at[0],
        recv_sem=w_sem.at[1],
        device_id=ahead,
        device_id_type=MESH,
    )
    w_copy.start()
    loads[0].wait()
    for b in range(input_blocks):
        tok_mine[b] = tok_in[:, b * BLOCK : (b + 1) * BLOCK]
    for copy in tok_copies:
        copy.start()
    for copy in cot_copies:
        copy.start()
    tok_own = pltpu.make_async_copy(tok_mine, tok_all.at[:, here], in_sem.at[0])
    tok_own.start()
    for load in loads[1:] + [tok_own]:
        load.wait()
    for copy in tok_copies + cot_copies:
        copy.wait()

    def moved_copy(j):
        return pltpu.make_async_remote_copy(
            src_ref=m_own.at[j],
            dst_ref=m_far.at[j],
            send_sem=m_send.at[j],
            recv_sem=m_recv.at[j],
            device_id=ahead,
            device_id_type=MESH,
        )

    def make_block(j):
        cols = pl.ds(pl.multiple_of(j * BLOCK, BLOCK), BLOCK)
        chosen = jnp.concatenate(
            [tok_all[pat_ref[k, j]].reshape(seq, BLOCK) for k in range(KB)], axis=1
        )
        packed = jnp.concatenate(
            [w_own[j, u].reshape(KB * BLOCK, BLOCK) for u in range(2)], axis=1
        )
        both = jnp.dot(chosen, packed, preferred_element_type=jnp.float32) * SCALE
        gate, up = both[:, :BLOCK], both[:, BLOCK:]
        sigma = jax.nn.sigmoid(gate)
        gated = gate * sigma
        hid_all[:, :, cols] = (gated * up).astype(jnp.bfloat16).reshape(groups, rows, BLOCK)
        back = cot_all[:, :, cols].reshape(seq, BLOCK).astype(jnp.float32)
        dgate = (back * up * sigma * (1.0 + gate * (1.0 - sigma))).astype(jnp.bfloat16)
        duptail = (back * gated).astype(jnp.bfloat16)
        tails = jnp.concatenate([dgate, duptail], axis=1)
        grad = (
            lax.dot_general(
                chosen, tails, (((0,), (0,)), ((), ())), preferred_element_type=jnp.float32
            )
            * SCALE
        )
        for u in range(2):
            old = m_own[j, u].reshape(KB * BLOCK, BLOCK).astype(jnp.float32)
            new = (0.9 * old + grad[:, u * BLOCK : (u + 1) * BLOCK]).astype(jnp.bfloat16)
            m_own[j, u] = new.reshape(KB, BLOCK, BLOCK)

    burst = min(FIRST, own_blocks)

    def make_and_send(j, carry):
        make_block(j)
        moved_copy(j).start()
        return carry

    def make_only(j, carry):
        make_block(j)
        return carry

    lax.fori_loop(0, burst, make_and_send, 0)
    lax.fori_loop(burst, own_blocks, make_only, 0)

    hid_copies = [
        pltpu.make_async_remote_copy(
            src_ref=hid_all.at[q],
            dst_ref=hid_out.at[:, own_columns(here)],
            send_sem=hid_send.at[i],
            recv_sem=hid_recv.at[i],
            device_id={"tensor": q},
            device_id_type=MESH,
        )
        for i, q in enumerate(peers)
    ]
    for copy in hid_copies:
        copy.start()
    hid_own = pltpu.make_async_copy(
        hid_all.at[here], hid_out.at[:, own_columns(here)], in_sem.at[0]
    )
    hid_own.start()

    w_copy.wait()

    def mix_block(j, carry):
        moved_copy(j).wait_send()
        later = j + AHEAD

        @pl.when(jnp.logical_and(later >= burst, later < own_blocks))
        def _():
            moved_copy(later).start()

        moved_copy(j).wait_recv()
        moved, far_moved = m_own[j], m_far[j]
        nw_out[j] = average(stepped_of(w_own[j], moved), stepped_of(w_far[j], far_moved))
        nm_out[j] = average(moved, far_moved)
        return carry

    lax.fori_loop(0, own_blocks, mix_block, 0)

    for copy in hid_copies:
        copy.wait()
    hid_own.wait()


def write_kernel(hid_ref, nw_ref, nm_ref, hid_out, nw_out, nm_out, sems):
    pairs = ((hid_ref, hid_out), (nw_ref, nw_out), (nm_ref, nm_out))
    copies = []
    for i, (src, dst) in enumerate(pairs):
        half = src.shape[0] // 2
        for k in range(2):
            part = pl.ds(k * half, half)
            copies.append(pltpu.make_async_copy(src.at[part], dst.at[part], sems.at[i, k]))
    for copy in copies:
        copy.start()
    for copy in copies:
        copy.wait()


def written(*results):
    held = [pltpu.with_memory_space_constraint(r, pltpu.VMEM) for r in results]
    return pl.pallas_call(
        write_kernel,
        out_shape=tuple(jax.ShapeDtypeStruct(r.shape, r.dtype) for r in results),
        in_specs=[pl.BlockSpec(memory_space=pltpu.VMEM)] * len(results),
        out_specs=(pl.BlockSpec(memory_space=pltpu.HBM),) * len(results),
        scratch_shapes=[pltpu.SemaphoreType.DMA((len(results), 2))],
        compiler_params=pltpu.CompilerParams(vmem_limit_bytes=1024 * 1024),
    )(*held)


def run(distance, replicas, groups, number, pattern, tokens, cotangent, weights, momentum):
    rows, model = tokens.shape
    own_blocks = weights.shape[0]
    width = own_blocks * BLOCK
    bf16 = jnp.bfloat16
    anywhere = pl.BlockSpec(memory_space=pl.ANY)
    others = groups - 1
    dma = pltpu.SemaphoreType.DMA
    results = pl.pallas_call(
        partial(kernel, distance, replicas, groups),
        out_shape=(
            pltpu.VMEM(cotangent.shape, bf16),
            pltpu.VMEM(weights.shape, bf16),
            pltpu.VMEM(weights.shape, bf16),
        ),
        in_specs=[anywhere] * 5,
        out_specs=(pl.BlockSpec(memory_space=pltpu.VMEM),) * 3,
        scratch_shapes=[
            pltpu.VMEM((rows, model), bf16),
            pltpu.VMEM((model // BLOCK, rows, BLOCK), bf16),
            pltpu.VMEM((model // BLOCK, groups, rows, BLOCK), bf16),
            pltpu.VMEM((groups, rows, width), bf16),
            pltpu.VMEM((groups, rows, width), bf16),
            pltpu.VMEM(weights.shape, bf16),
            pltpu.VMEM(weights.shape, bf16),
            pltpu.VMEM(weights.shape, bf16),
            pltpu.VMEM(weights.shape, bf16),
            pltpu.SMEM(pattern.shape, jnp.int32),
            dma((5,)),
            dma((2,)),
            dma((own_blocks,)),
            dma((own_blocks,)),
            dma((others,)),
            dma((others,)),
            dma((others,)),
            dma((others,)),
            dma((others,)),
            dma((others,)),
        ],
        compiler_params=pltpu.CompilerParams(
            collective_id=number, has_side_effects=True, vmem_limit_bytes=42 * 1024 * 1024
        ),
        cost_estimate=pl.CostEstimate(
            flops=8 * groups * rows * KB * BLOCK * width,
            bytes_accessed=2 * (groups * rows * model + 6 * weights.size),
            transcendentals=groups * rows * width,
        ),
    )(pattern, tokens, cotangent, weights, momentum)
    return written(*results)


def per_device(tokens, cotangent, weights, momentum, pattern, step):
    replicas = lax.axis_size("dp")
    groups = lax.axis_size("tensor")
    levels = replicas.bit_length() - 1
    branches = [partial(run, 2**level, replicas, groups, level) for level in range(levels)]
    hidden, new_weights, new_momentum = lax.switch(
        lax.rem(step, levels), branches, pattern.T, tokens[0], cotangent[0], weights[0], momentum[0]
    )
    return (hidden[None], new_weights[None], new_momentum[None])


def solution(mesh):
    in_specs = (
        P("dp", "tensor", None),
        P("dp", "tensor", None),
        P("dp", "tensor", None, None, None, None),
        P("dp", "tensor", None, None, None, None),
        P("tensor", None),
        P(),
    )
    out_specs = (
        P("dp", "tensor", None),
        P("dp", "tensor", None, None, None, None),
        P("dp", "tensor", None, None, None, None),
    )
    return jax.shard_map(
        per_device, mesh=mesh, in_specs=in_specs, out_specs=out_specs, check_vma=False
    )
```

```python
from functools import partial

import jax
import jax.numpy as jnp
from jax import lax
from jax.experimental import pallas as pl
from jax.experimental.pallas import tpu as pltpu
from jax.sharding import PartitionSpec as P

BLOCK = 128
KB = 2
SCALE = (KB * BLOCK) ** (-0.5)
MESH = pl.DeviceIdType.MESH
FIRST = 10
AHEAD = 4


def stepped_of(packed, moved):
    return (packed.astype(jnp.float32) - 0.1 * moved.astype(jnp.float32)).astype(jnp.bfloat16)


def average(one, other):
    return ((one.astype(jnp.float32) + other.astype(jnp.float32)) * 0.5).astype(jnp.bfloat16)


def kernel(
    distance,
    replicas,
    groups,
    pat_hbm,
    tok_ref,
    cot_ref,
    w_ref,
    m_ref,
    hid_out,
    nw_out,
    nm_out,
    tok_in,
    tok_mine,
    tok_all,
    cot_all,
    hid_all,
    w_own,
    m_own,
    w_far,
    m_far,
    pat_ref,
    in_sem,
    w_sem,
    m_send,
    m_recv,
    tok_send,
    tok_recv,
    cot_send,
    cot_recv,
    hid_send,
    hid_recv,
):
    own_blocks = w_ref.shape[0]
    rows = tok_ref.shape[0]
    input_blocks = tok_ref.shape[1] // BLOCK
    width = own_blocks * BLOCK
    seq = rows * groups
    here = lax.axis_index("tensor")
    replica = lax.axis_index("dp")
    ahead = {"dp": lax.rem(replica + distance, replicas)}
    behind = {"dp": lax.rem(replica + replicas - distance, replicas)}
    peers = [lax.rem(here + o, groups) for o in range(1, groups)]

    barrier = pltpu.get_barrier_semaphore()
    greeted = [behind] + [{"tensor": q} for q in peers]
    if 2 * distance != replicas:
        greeted.append(ahead)
    for device in greeted:
        pl.semaphore_signal(barrier, inc=1, device_id=device, device_id_type=MESH)

    def own_columns(q):
        return pl.ds(pl.multiple_of(q * width, BLOCK), width)

    loads = [
        pltpu.make_async_copy(tok_ref, tok_in, in_sem.at[0]),
        pltpu.make_async_copy(cot_ref.at[:, own_columns(here)], cot_all.at[here], in_sem.at[1]),
        pltpu.make_async_copy(w_ref, w_own, in_sem.at[2]),
        pltpu.make_async_copy(m_ref, m_own, in_sem.at[3]),
        pltpu.make_async_copy(pat_hbm, pat_ref, in_sem.at[4]),
    ]
    for load in loads:
        load.start()
    pl.semaphore_wait(barrier, len(greeted))

    tok_copies = [
        pltpu.make_async_remote_copy(
            src_ref=tok_mine,
            dst_ref=tok_all.at[:, here],
            send_sem=tok_send.at[i],
            recv_sem=tok_recv.at[i],
            device_id={"tensor": q},
            device_id_type=MESH,
        )
        for i, q in enumerate(peers)
    ]
    cot_copies = [
        pltpu.make_async_remote_copy(
            src_ref=cot_ref.at[:, own_columns(q)],
            dst_ref=cot_all.at[here],
            send_sem=cot_send.at[i],
            recv_sem=cot_recv.at[i],
            device_id={"tensor": q},
            device_id_type=MESH,
        )
        for i, q in enumerate(peers)
    ]
    w_copy = pltpu.make_async_remote_copy(
        src_ref=w_ref,
        dst_ref=w_far,
        send_sem=w_sem.at[0],
        recv_sem=w_sem.at[1],
        device_id=ahead,
        device_id_type=MESH,
    )
    w_copy.start()
    loads[0].wait()
    for b in range(input_blocks):
        tok_mine[b] = tok_in[:, b * BLOCK : (b + 1) * BLOCK]
    for copy in tok_copies:
        copy.start()
    for copy in cot_copies:
        copy.start()
    tok_own = pltpu.make_async_copy(tok_mine, tok_all.at[:, here], in_sem.at[0])
    tok_own.start()
    for load in loads[1:] + [tok_own]:
        load.wait()
    for copy in tok_copies + cot_copies:
        copy.wait()

    def moved_copy(j):
        return pltpu.make_async_remote_copy(
            src_ref=m_own.at[j],
            dst_ref=m_far.at[j],
            send_sem=m_send.at[j],
            recv_sem=m_recv.at[j],
            device_id=ahead,
            device_id_type=MESH,
        )

    def make_block(j):
        cols = pl.ds(pl.multiple_of(j * BLOCK, BLOCK), BLOCK)
        chosen = jnp.concatenate(
            [tok_all[pat_ref[k, j]].reshape(seq, BLOCK) for k in range(KB)], axis=1
        )
        packed = jnp.concatenate(
            [w_own[j, u].reshape(KB * BLOCK, BLOCK) for u in range(2)], axis=1
        )
        both = jnp.dot(chosen, packed, preferred_element_type=jnp.float32) * SCALE
        gate, up = both[:, :BLOCK], both[:, BLOCK:]
        sigma = jax.nn.sigmoid(gate)
        gated = gate * sigma
        hid_all[:, :, cols] = (gated * up).astype(jnp.bfloat16).reshape(groups, rows, BLOCK)
        back = cot_all[:, :, cols].reshape(seq, BLOCK).astype(jnp.float32)
        dgate = (back * up * sigma * (1.0 + gate * (1.0 - sigma))).astype(jnp.bfloat16)
        duptail = (back * gated).astype(jnp.bfloat16)
        tails = jnp.concatenate([dgate, duptail], axis=1)
        grad = (
            lax.dot_general(
                chosen, tails, (((0,), (0,)), ((), ())), preferred_element_type=jnp.float32
            )
            * SCALE
        )
        for u in range(2):
            old = m_own[j, u].reshape(KB * BLOCK, BLOCK).astype(jnp.float32)
            new = (0.9 * old + grad[:, u * BLOCK : (u + 1) * BLOCK]).astype(jnp.bfloat16)
            m_own[j, u] = new.reshape(KB, BLOCK, BLOCK)

    burst = min(FIRST, own_blocks)

    def make_and_send(j, carry):
        make_block(j)
        moved_copy(j).start()
        return carry

    def make_only(j, carry):
        make_block(j)
        return carry

    lax.fori_loop(0, burst, make_and_send, 0)
    lax.fori_loop(burst, own_blocks, make_only, 0)

    hid_copies = [
        pltpu.make_async_remote_copy(
            src_ref=hid_all.at[q],
            dst_ref=hid_out.at[:, own_columns(here)],
            send_sem=hid_send.at[i],
            recv_sem=hid_recv.at[i],
            device_id={"tensor": q},
            device_id_type=MESH,
        )
        for i, q in enumerate(peers)
    ]
    for copy in hid_copies:
        copy.start()
    hid_own = pltpu.make_async_copy(
        hid_all.at[here], hid_out.at[:, own_columns(here)], in_sem.at[0]
    )
    hid_own.start()

    w_copy.wait()

    def mix_block(j, carry):
        moved_copy(j).wait_send()
        later = j + AHEAD

        @pl.when(jnp.logical_and(later >= burst, later < own_blocks))
        def _():
            moved_copy(later).start()

        moved_copy(j).wait_recv()
        moved, far_moved = m_own[j], m_far[j]
        nw_out[j] = average(stepped_of(w_own[j], moved), stepped_of(w_far[j], far_moved))
        nm_out[j] = average(moved, far_moved)
        return carry

    lax.fori_loop(0, own_blocks, mix_block, 0)

    for copy in hid_copies:
        copy.wait()
    hid_own.wait()


def pieces_of(array):
    unit = 16 if len(array.shape) == 2 else 1
    return max(k for k in (1, 2, 4) if array.shape[0] % (k * unit) == 0)


def write_kernel(hid_ref, nw_ref, nm_ref, hid_out, nw_out, nm_out, sems):
    pairs = ((hid_ref, hid_out), (nw_ref, nw_out), (nm_ref, nm_out))
    copies = []
    for i, (src, dst) in enumerate(pairs):
        pieces = pieces_of(src)
        size = src.shape[0] // pieces
        for k in range(pieces):
            part = pl.ds(k * size, size)
            copies.append(pltpu.make_async_copy(src.at[part], dst.at[part], sems.at[i, k]))
    for copy in copies:
        copy.start()
    for copy in copies:
        copy.wait()


def written(*results):
    held = [pltpu.with_memory_space_constraint(r, pltpu.VMEM) for r in results]
    return pl.pallas_call(
        write_kernel,
        out_shape=tuple(jax.ShapeDtypeStruct(r.shape, r.dtype) for r in results),
        in_specs=[pl.BlockSpec(memory_space=pltpu.VMEM)] * len(results),
        out_specs=(pl.BlockSpec(memory_space=pltpu.HBM),) * len(results),
        scratch_shapes=[pltpu.SemaphoreType.DMA((len(results), 4))],
        compiler_params=pltpu.CompilerParams(vmem_limit_bytes=1024 * 1024),
    )(*held)


def run(distance, replicas, groups, number, pattern, tokens, cotangent, weights, momentum):
    rows, model = tokens.shape
    own_blocks = weights.shape[0]
    width = own_blocks * BLOCK
    bf16 = jnp.bfloat16
    anywhere = pl.BlockSpec(memory_space=pl.ANY)
    others = groups - 1
    dma = pltpu.SemaphoreType.DMA
    results = pl.pallas_call(
        partial(kernel, distance, replicas, groups),
        out_shape=(
            pltpu.VMEM(cotangent.shape, bf16),
            pltpu.VMEM(weights.shape, bf16),
            pltpu.VMEM(weights.shape, bf16),
        ),
        in_specs=[anywhere] * 5,
        out_specs=(pl.BlockSpec(memory_space=pltpu.VMEM),) * 3,
        scratch_shapes=[
            pltpu.VMEM((rows, model), bf16),
            pltpu.VMEM((model // BLOCK, rows, BLOCK), bf16),
            pltpu.VMEM((model // BLOCK, groups, rows, BLOCK), bf16),
            pltpu.VMEM((groups, rows, width), bf16),
            pltpu.VMEM((groups, rows, width), bf16),
            pltpu.VMEM(weights.shape, bf16),
            pltpu.VMEM(weights.shape, bf16),
            pltpu.VMEM(weights.shape, bf16),
            pltpu.VMEM(weights.shape, bf16),
            pltpu.SMEM(pattern.shape, jnp.int32),
            dma((5,)),
            dma((2,)),
            dma((own_blocks,)),
            dma((own_blocks,)),
            dma((others,)),
            dma((others,)),
            dma((others,)),
            dma((others,)),
            dma((others,)),
            dma((others,)),
        ],
        compiler_params=pltpu.CompilerParams(
            collective_id=number, has_side_effects=True, vmem_limit_bytes=42 * 1024 * 1024
        ),
        cost_estimate=pl.CostEstimate(
            flops=8 * groups * rows * KB * BLOCK * width,
            bytes_accessed=2 * (groups * rows * model + 6 * weights.size),
            transcendentals=groups * rows * width,
        ),
    )(pattern, tokens, cotangent, weights, momentum)
    return written(*results)


def per_device(tokens, cotangent, weights, momentum, pattern, step):
    replicas = lax.axis_size("dp")
    groups = lax.axis_size("tensor")
    levels = replicas.bit_length() - 1
    branches = [partial(run, 2**level, replicas, groups, level) for level in range(levels)]
    hidden, new_weights, new_momentum = lax.switch(
        lax.rem(step, levels), branches, pattern.T, tokens[0], cotangent[0], weights[0], momentum[0]
    )
    return (hidden[None], new_weights[None], new_momentum[None])


def solution(mesh):
    in_specs = (
        P("dp", "tensor", None),
        P("dp", "tensor", None),
        P("dp", "tensor", None, None, None, None),
        P("dp", "tensor", None, None, None, None),
        P("tensor", None),
        P(),
    )
    out_specs = (
        P("dp", "tensor", None),
        P("dp", "tensor", None, None, None, None),
        P("dp", "tensor", None, None, None, None),
    )
    return jax.shard_map(
        per_device, mesh=mesh, in_specs=in_specs, out_specs=out_specs, check_vma=False
    )
```

```python
from functools import partial

import jax
import jax.numpy as jnp
from jax import lax
from jax.experimental import pallas as pl
from jax.experimental.pallas import tpu as pltpu
from jax.sharding import PartitionSpec as P

BLOCK = 128
KB = 2
SCALE = (KB * BLOCK) ** (-0.5)
MESH = pl.DeviceIdType.MESH
FIRST = 10
AHEAD = 4


def stepped_of(packed, moved):
    return (packed.astype(jnp.float32) - 0.1 * moved.astype(jnp.float32)).astype(jnp.bfloat16)


def average(one, other):
    return ((one.astype(jnp.float32) + other.astype(jnp.float32)) * 0.5).astype(jnp.bfloat16)


def kernel(
    distance,
    replicas,
    groups,
    pat_hbm,
    tok_ref,
    cot_ref,
    w_ref,
    m_ref,
    hid_out,
    nw_out,
    nm_out,
    tok_in,
    tok_mine,
    tok_all,
    cot_all,
    hid_all,
    w_own,
    m_own,
    w_far,
    m_far,
    pat_ref,
    in_sem,
    w_sem,
    m_send,
    m_recv,
    tok_send,
    tok_recv,
    cot_send,
    cot_recv,
    hid_send,
    hid_recv,
):
    own_blocks = w_ref.shape[0]
    rows = tok_ref.shape[0]
    input_blocks = tok_ref.shape[1] // BLOCK
    width = own_blocks * BLOCK
    seq = rows * groups
    here = lax.axis_index("tensor")
    replica = lax.axis_index("dp")
    ahead = {"dp": lax.rem(replica + distance, replicas)}
    behind = {"dp": lax.rem(replica + replicas - distance, replicas)}
    peers = [lax.rem(here + o, groups) for o in range(1, groups)]

    barrier = pltpu.get_barrier_semaphore()
    greeted = [behind] + [{"tensor": q} for q in peers]
    if 2 * distance != replicas:
        greeted.append(ahead)
    for device in greeted:
        pl.semaphore_signal(barrier, inc=1, device_id=device, device_id_type=MESH)

    def own_columns(q):
        return pl.ds(pl.multiple_of(q * width, BLOCK), width)

    loads = [
        pltpu.make_async_copy(tok_ref, tok_in, in_sem.at[0]),
        pltpu.make_async_copy(cot_ref.at[:, own_columns(here)], cot_all.at[here], in_sem.at[1]),
        pltpu.make_async_copy(w_ref, w_own, in_sem.at[2]),
        pltpu.make_async_copy(m_ref, m_own, in_sem.at[3]),
        pltpu.make_async_copy(pat_hbm, pat_ref, in_sem.at[4]),
    ]
    for load in loads:
        load.start()
    pl.semaphore_wait(barrier, len(greeted))

    tok_copies = [
        pltpu.make_async_remote_copy(
            src_ref=tok_mine,
            dst_ref=tok_all.at[:, here],
            send_sem=tok_send.at[i],
            recv_sem=tok_recv.at[i],
            device_id={"tensor": q},
            device_id_type=MESH,
        )
        for i, q in enumerate(peers)
    ]
    cot_copies = [
        pltpu.make_async_remote_copy(
            src_ref=cot_ref.at[:, own_columns(q)],
            dst_ref=cot_all.at[here],
            send_sem=cot_send.at[i],
            recv_sem=cot_recv.at[i],
            device_id={"tensor": q},
            device_id_type=MESH,
        )
        for i, q in enumerate(peers)
    ]
    w_pieces = pieces_of(w_ref)
    w_size = own_blocks // w_pieces
    w_copies = [
        pltpu.make_async_remote_copy(
            src_ref=w_ref.at[pl.ds(k * w_size, w_size)],
            dst_ref=w_far.at[pl.ds(k * w_size, w_size)],
            send_sem=w_sem.at[0, k],
            recv_sem=w_sem.at[1, k],
            device_id=ahead,
            device_id_type=MESH,
        )
        for k in range(w_pieces)
    ]
    for copy in w_copies:
        copy.start()
    loads[0].wait()
    for b in range(input_blocks):
        tok_mine[b] = tok_in[:, b * BLOCK : (b + 1) * BLOCK]
    for copy in tok_copies:
        copy.start()
    for copy in cot_copies:
        copy.start()
    tok_own = pltpu.make_async_copy(tok_mine, tok_all.at[:, here], in_sem.at[0])
    tok_own.start()
    for load in loads[1:] + [tok_own]:
        load.wait()
    for copy in tok_copies + cot_copies:
        copy.wait()

    def moved_copy(j):
        return pltpu.make_async_remote_copy(
            src_ref=m_own.at[j],
            dst_ref=m_far.at[j],
            send_sem=m_send.at[j],
            recv_sem=m_recv.at[j],
            device_id=ahead,
            device_id_type=MESH,
        )

    def make_block(j):
        cols = pl.ds(pl.multiple_of(j * BLOCK, BLOCK), BLOCK)
        chosen = jnp.concatenate(
            [tok_all[pat_ref[k, j]].reshape(seq, BLOCK) for k in range(KB)], axis=1
        )
        packed = jnp.concatenate(
            [w_own[j, u].reshape(KB * BLOCK, BLOCK) for u in range(2)], axis=1
        )
        both = jnp.dot(chosen, packed, preferred_element_type=jnp.float32) * SCALE
        gate, up = both[:, :BLOCK], both[:, BLOCK:]
        sigma = jax.nn.sigmoid(gate)
        gated = gate * sigma
        hid_all[:, :, cols] = (gated * up).astype(jnp.bfloat16).reshape(groups, rows, BLOCK)
        back = cot_all[:, :, cols].reshape(seq, BLOCK).astype(jnp.float32)
        dgate = (back * up * sigma * (1.0 + gate * (1.0 - sigma))).astype(jnp.bfloat16)
        duptail = (back * gated).astype(jnp.bfloat16)
        tails = jnp.concatenate([dgate, duptail], axis=1)
        grad = (
            lax.dot_general(
                chosen, tails, (((0,), (0,)), ((), ())), preferred_element_type=jnp.float32
            )
            * SCALE
        )
        for u in range(2):
            old = m_own[j, u].reshape(KB * BLOCK, BLOCK).astype(jnp.float32)
            new = (0.9 * old + grad[:, u * BLOCK : (u + 1) * BLOCK]).astype(jnp.bfloat16)
            m_own[j, u] = new.reshape(KB, BLOCK, BLOCK)

    burst = min(FIRST, own_blocks)

    def make_and_send(j, carry):
        make_block(j)
        moved_copy(j).start()
        return carry

    def make_only(j, carry):
        make_block(j)
        return carry

    lax.fori_loop(0, burst, make_and_send, 0)
    lax.fori_loop(burst, own_blocks, make_only, 0)

    hid_copies = [
        pltpu.make_async_remote_copy(
            src_ref=hid_all.at[q],
            dst_ref=hid_out.at[:, own_columns(here)],
            send_sem=hid_send.at[i],
            recv_sem=hid_recv.at[i],
            device_id={"tensor": q},
            device_id_type=MESH,
        )
        for i, q in enumerate(peers)
    ]
    for copy in hid_copies:
        copy.start()
    hid_own = pltpu.make_async_copy(
        hid_all.at[here], hid_out.at[:, own_columns(here)], in_sem.at[0]
    )
    hid_own.start()

    for copy in w_copies:
        copy.wait()

    def mix_block(j, carry):
        moved_copy(j).wait_send()
        later = j + AHEAD

        @pl.when(jnp.logical_and(later >= burst, later < own_blocks))
        def _():
            moved_copy(later).start()

        moved_copy(j).wait_recv()
        moved, far_moved = m_own[j], m_far[j]
        nw_out[j] = average(stepped_of(w_own[j], moved), stepped_of(w_far[j], far_moved))
        nm_out[j] = average(moved, far_moved)
        return carry

    lax.fori_loop(0, own_blocks, mix_block, 0)

    for copy in hid_copies:
        copy.wait()
    hid_own.wait()


def pieces_of(array):
    unit = 16 if len(array.shape) == 2 else 1
    return max(k for k in (1, 2, 4) if array.shape[0] % (k * unit) == 0)


def write_kernel(hid_ref, nw_ref, nm_ref, hid_out, nw_out, nm_out, sems):
    pairs = ((hid_ref, hid_out), (nw_ref, nw_out), (nm_ref, nm_out))
    copies = []
    for i, (src, dst) in enumerate(pairs):
        pieces = pieces_of(src)
        size = src.shape[0] // pieces
        for k in range(pieces):
            part = pl.ds(k * size, size)
            copies.append(pltpu.make_async_copy(src.at[part], dst.at[part], sems.at[i, k]))
    for copy in copies:
        copy.start()
    for copy in copies:
        copy.wait()


def written(*results):
    held = [pltpu.with_memory_space_constraint(r, pltpu.VMEM) for r in results]
    return pl.pallas_call(
        write_kernel,
        out_shape=tuple(jax.ShapeDtypeStruct(r.shape, r.dtype) for r in results),
        in_specs=[pl.BlockSpec(memory_space=pltpu.VMEM)] * len(results),
        out_specs=(pl.BlockSpec(memory_space=pltpu.HBM),) * len(results),
        scratch_shapes=[pltpu.SemaphoreType.DMA((len(results), 4))],
        compiler_params=pltpu.CompilerParams(vmem_limit_bytes=1024 * 1024),
    )(*held)


def run(distance, replicas, groups, number, pattern, tokens, cotangent, weights, momentum):
    rows, model = tokens.shape
    own_blocks = weights.shape[0]
    width = own_blocks * BLOCK
    bf16 = jnp.bfloat16
    anywhere = pl.BlockSpec(memory_space=pl.ANY)
    others = groups - 1
    dma = pltpu.SemaphoreType.DMA
    results = pl.pallas_call(
        partial(kernel, distance, replicas, groups),
        out_shape=(
            pltpu.VMEM(cotangent.shape, bf16),
            pltpu.VMEM(weights.shape, bf16),
            pltpu.VMEM(weights.shape, bf16),
        ),
        in_specs=[anywhere] * 5,
        out_specs=(pl.BlockSpec(memory_space=pltpu.VMEM),) * 3,
        scratch_shapes=[
            pltpu.VMEM((rows, model), bf16),
            pltpu.VMEM((model // BLOCK, rows, BLOCK), bf16),
            pltpu.VMEM((model // BLOCK, groups, rows, BLOCK), bf16),
            pltpu.VMEM((groups, rows, width), bf16),
            pltpu.VMEM((groups, rows, width), bf16),
            pltpu.VMEM(weights.shape, bf16),
            pltpu.VMEM(weights.shape, bf16),
            pltpu.VMEM(weights.shape, bf16),
            pltpu.VMEM(weights.shape, bf16),
            pltpu.SMEM(pattern.shape, jnp.int32),
            dma((5,)),
            dma((2, 4)),
            dma((own_blocks,)),
            dma((own_blocks,)),
            dma((others,)),
            dma((others,)),
            dma((others,)),
            dma((others,)),
            dma((others,)),
            dma((others,)),
        ],
        compiler_params=pltpu.CompilerParams(
            collective_id=number, has_side_effects=True, vmem_limit_bytes=42 * 1024 * 1024
        ),
        cost_estimate=pl.CostEstimate(
            flops=8 * groups * rows * KB * BLOCK * width,
            bytes_accessed=2 * (groups * rows * model + 6 * weights.size),
            transcendentals=groups * rows * width,
        ),
    )(pattern, tokens, cotangent, weights, momentum)
    return written(*results)


def per_device(tokens, cotangent, weights, momentum, pattern, step):
    replicas = lax.axis_size("dp")
    groups = lax.axis_size("tensor")
    levels = replicas.bit_length() - 1
    branches = [partial(run, 2**level, replicas, groups, level) for level in range(levels)]
    hidden, new_weights, new_momentum = lax.switch(
        lax.rem(step, levels), branches, pattern.T, tokens[0], cotangent[0], weights[0], momentum[0]
    )
    return (hidden[None], new_weights[None], new_momentum[None])


def solution(mesh):
    in_specs = (
        P("dp", "tensor", None),
        P("dp", "tensor", None),
        P("dp", "tensor", None, None, None, None),
        P("dp", "tensor", None, None, None, None),
        P("tensor", None),
        P(),
    )
    out_specs = (
        P("dp", "tensor", None),
        P("dp", "tensor", None, None, None, None),
        P("dp", "tensor", None, None, None, None),
    )
    return jax.shard_map(
        per_device, mesh=mesh, in_specs=in_specs, out_specs=out_specs, check_vma=False
    )
```
